32 devices in a mesh: member: 2 (over x), region: 16 (over z, y, core).
Axes of the slice: x: 2, y: 2, z: 4, core: 2. Of those that a mesh axis runs over, the one named last changes fastest.
Arguments:
- grid_latent: bfloat16 [32768, 512], P(('member', 'region')), parts along dimension 0, may hold values from -6 to 6
- edge_latent: bfloat16 [98304, 512], P(('member', 'region')), parts along dimension 0, may hold values from -6 to 6
- mesh_latent: bfloat16 [8192, 512], P(('member', 'region')), parts along dimension 0, may hold values from -6 to 6
- sources: int32 [16384, 3], P('region'), may hold values from 0 to 4095, as said below
- w_src: bfloat16 [512, 512], replicated, may hold values from -0.25 to 0.25
- w_edge: bfloat16 [512, 512], replicated, may hold values from -0.25 to 0.25
- w_dst: bfloat16 [512, 512], replicated, may hold values from -0.25 to 0.25
- bias: float32 [512], replicated, may hold values from -3 to 3
- w_out: bfloat16 [512, 84], replicated, may hold values from -0.25 to 0.25
- cotangent: bfloat16 [32768, 84], P(('member', 'region')), parts along dimension 0, may hold values from -6 to 6
Outputs:
- d_grid: bfloat16 [32768, 512], P(('member', 'region')), parts along dimension 0
- d_mesh: float32 [8192, 512], P(('member', 'region')), parts along dimension 0
- d_w_src: float32 [1024, 512], P('member'), parts along dimension 0
- d_w_edge: float32 [1024, 512], P('member'), parts along dimension 0
- d_w_dst: float32 [1024, 512], P('member'), parts along dimension 0
- d_bias: float32 [1024], P('member'), parts along dimension 0
- d_w_out: float32 [1024, 84], P('member'), parts along dimension 0
The draws below stay inside these ranges and needn't reach their ends.
There are 2 independent parts, one for each index of `member`. The reference program is written for one: setup_inputs(seed, part) draws one part's arguments, and reference() takes and returns one part's arrays. A program takes and returns all parts, laid end to end along the dimension named above; an argument that names none is the same for every part. Nothing has to cross between parts.
Inputs may be any that keep to these rules, and one draw needn't show every extreme that they name: `sources`: A grid node g of region r = g // 1024 names only mesh nodes of regions r - 1, r and r + 1 taken cyclically over the regions, where mesh node m lies in region m // 256.
All inputs are finite; a program needn't handle non-finite values.
Results may differ from the reference program's by a relative error of at most 0.012.
Values may be sent and summed in bfloat16 or wider, within the bound.
No kernel may reach another device: no remote copies, remote signals or barrier semaphores. Data moves between devices by JAX's collectives and lax.ppermute only.
A program may use at most 128 MiB of HBM per device.

```python
import jax
import jax.numpy as jnp
from jax import lax

D = 512
OUT = 84
FAN = 3
G_DEV = 1024
M_DEV = 256
GRID = 16384
MESH = 4096
EDGES = 49152


def draw_sources(key, part):
    key = jax.random.fold_in(key, 7)
    first, second = jax.random.split(key)
    count = MESH // M_DEV
    region = (jnp.arange(GRID * FAN, dtype=jnp.int32) // (FAN * G_DEV)).reshape(GRID, FAN)
    offset = jax.random.randint(first, (GRID, FAN), -1, 2, dtype=jnp.int32)
    inside = jax.random.randint(second, (GRID, FAN), 0, M_DEV, dtype=jnp.int32)
    return (jnp.mod(region + offset, count) * M_DEV + inside).astype(jnp.int32)


def block_levels(rng, dims, pieces, smallest, largest):
    def one(position, parts):
        steps = jax.random.uniform(jax.random.fold_in(jax.random.fold_in(rng, 6), position), (parts,), jnp.float32, smallest / len(pieces), largest / len(pieces))
        return jnp.repeat(jnp.exp(steps), dims[position] // parts).reshape((-1,) + (1,) * (len(dims) - position - 1))

    factor_of = one(*pieces[0])
    for cut in pieces[1:]:
        factor_of = factor_of * one(*cut)
    return factor_of


def scatter_about(rng, dims, spread, bound, cuts=(), held_as=jnp.bfloat16):
    level = block_levels(rng, dims, cuts, -0.22, 0.18) if cuts else 1.0
    result = jax.random.normal(rng, dims, jnp.float32) * spread * level
    return jnp.minimum(jnp.maximum(result, -bound), bound).astype(held_as)


def setup_inputs(seed: int = 0, part: int = 0) -> dict:
    splits = jax.random.split(jax.random.key(seed), 11)
    part_splits = jax.random.split(jax.random.fold_in(splits[10], part), 11)
    grid_latent = scatter_about(part_splits[0], (GRID, D), 1.0, 6.0, ((0, 16),))
    edge_latent = scatter_about(part_splits[1], (EDGES, D), 1.0, 6.0, ((0, 16),))
    mesh_latent = scatter_about(part_splits[2], (MESH, D), 1.0, 6.0, ((0, 16),))
    sources = draw_sources(jax.random.fold_in(splits[10], 71), part)
    w_src = scatter_about(splits[4], (D, D), D ** -0.5, 0.25)
    w_edge = scatter_about(splits[5], (D, D), D ** -0.5, 0.25)
    w_dst = scatter_about(splits[6], (D, D), D ** -0.5, 0.25)
    bias = scatter_about(splits[7], (D,), 0.5, 3.0, (), jnp.float32)
    w_out = scatter_about(splits[8], (D, OUT), D ** -0.5, 0.25)
    cotangent = scatter_about(part_splits[9], (GRID, OUT), 1.0, 6.0, ((0, 16),))
    return dict(grid_latent=grid_latent, edge_latent=edge_latent, mesh_latent=mesh_latent, sources=sources, w_src=w_src, w_edge=w_edge, w_dst=w_dst, bias=bias, w_out=w_out, cotangent=cotangent)


def reference(grid_latent, edge_latent, mesh_latent, sources, w_src, w_edge, w_dst, bias, w_out, cotangent):
    blocks = GRID // G_DEV
    grid_b = grid_latent.reshape(blocks, G_DEV, D)
    edge_b = edge_latent.reshape(blocks, FAN * G_DEV, D)
    src_b = sources.reshape(blocks, G_DEV * FAN)
    cot_b = cotangent.reshape(blocks, G_DEV, OUT)

    def step(carry, items):
        g_src, g_edge, g_dst, g_bias, g_out, g_mesh = carry
        grid_rows, edge_rows, src_idx, cot_rows = items
        src_rows = mesh_latent[src_idx]
        node_term = jnp.dot(grid_rows, w_dst, preferred_element_type=jnp.float32)
        pre = (jnp.dot(src_rows, w_src, preferred_element_type=jnp.float32)
               + jnp.dot(edge_rows, w_edge, preferred_element_type=jnp.float32)
               + jnp.repeat(node_term, FAN, axis=0) + bias)
        sig = jax.nn.sigmoid(pre)
        agg = jnp.sum((pre * sig).reshape(G_DEV, FAN, D), axis=1).astype(jnp.bfloat16)
        d_agg = jnp.dot(cot_rows, w_out.T, preferred_element_type=jnp.float32).astype(jnp.bfloat16)
        g_out = g_out + jnp.dot(agg.T, cot_rows, preferred_element_type=jnp.float32)
        slope = sig * (1.0 + pre * (1.0 - sig))
        d_pre = (jnp.repeat(d_agg.astype(jnp.float32), FAN, axis=0) * slope).astype(jnp.bfloat16)
        d_node = jnp.sum(d_pre.astype(jnp.float32).reshape(G_DEV, FAN, D), axis=1).astype(jnp.bfloat16)
        g_src = g_src + jnp.dot(src_rows.T, d_pre, preferred_element_type=jnp.float32)
        g_edge = g_edge + jnp.dot(edge_rows.T, d_pre, preferred_element_type=jnp.float32)
        g_dst = g_dst + jnp.dot(grid_rows.T, d_node, preferred_element_type=jnp.float32)
        g_bias = g_bias + jnp.sum(d_pre.astype(jnp.float32), axis=0)
        mesh_term = jnp.dot(d_pre, w_src.T, preferred_element_type=jnp.float32)
        g_mesh = g_mesh.at[src_idx].add(mesh_term)
        d_grid = jnp.dot(d_node, w_dst.T, preferred_element_type=jnp.float32).astype(jnp.bfloat16)
        return (g_src, g_edge, g_dst, g_bias, g_out, g_mesh), d_grid

    zero_sq = jnp.zeros((D, D), jnp.float32)
    init = (zero_sq, zero_sq, zero_sq, jnp.zeros((D,), jnp.float32),
            jnp.zeros((D, OUT), jnp.float32), jnp.zeros((MESH, D), jnp.float32))
    carry, d_grid = lax.scan(step, init, (grid_b, edge_b, src_b, cot_b))
    g_src, g_edge, g_dst, g_bias, g_out, g_mesh = carry
    return (d_grid.reshape(GRID, D), g_mesh, g_src, g_edge, g_dst, g_bias, g_out)
```

```python
import functools

import jax
import jax.numpy as jnp
from jax import lax
from jax.experimental import pallas as pl
from jax.experimental.pallas import tpu as pltpu
from jax.sharding import PartitionSpec as P

BF16 = jnp.bfloat16
F32 = jnp.float32
TILE = 256
NT = (((1,), (1,)), ((), ()))
TN = (((0,), (0,)), ((), ()))
VMEM_LIMIT = 40 * 1024 * 1024


def dot(a, b, dims=(((1,), (0,)), ((), ()))):
    return lax.dot_general(a, b, dims, preferred_element_type=F32)


def params():
    return pltpu.CompilerParams(vmem_limit_bytes=VMEM_LIMIT)


def base_kernel(fan, edge, grid, cot, w_edge, w_dst, w_out, bias, planes, base, d_agg, wide):
    lanes = wide.shape[2]
    for c in range(wide.shape[0]):
        wide[c] = edge[:, c * lanes : (c + 1) * lanes].astype(F32)
    node = dot(grid[...], w_dst[...]) + bias[...]
    rows = grid.shape[0]
    for k in range(fan):
        pieces = [wide[c, pl.ds(k, rows, stride=fan), :] for c in range(wide.shape[0])]
        plane = jnp.concatenate(pieces, axis=1).astype(BF16)
        planes[k] = plane
        base[k] = node
        base[k] += dot(plane, w_edge[...])
    d_agg[...] = dot(cot[...], w_out[...], NT).astype(BF16)


def base_call(edge, grid, cot, w_edge, w_dst, w_out, bias):
    nodes, width = grid.shape
    fan = edge.shape[0] // nodes
    outs = cot.shape[1]
    whole = lambda *shape: pl.BlockSpec(shape, lambda i: (0,) * len(shape))
    return pl.pallas_call(
        functools.partial(base_kernel, fan),
        grid=(nodes // TILE,),
        in_specs=[
            pl.BlockSpec((fan * TILE, width), lambda i: (i, 0)),
            pl.BlockSpec((TILE, width), lambda i: (i, 0)),
            pl.BlockSpec((TILE, outs), lambda i: (i, 0)),
            whole(width, width),
            whole(width, width),
            whole(width, outs),
            whole(1, width),
        ],
        out_specs=[
            pl.BlockSpec((fan, TILE, width), lambda i: (0, i, 0)),
            pl.BlockSpec((fan, TILE, width), lambda i: (0, i, 0)),
            pl.BlockSpec((TILE, width), lambda i: (i, 0)),
        ],
        out_shape=[
            jax.ShapeDtypeStruct((fan, nodes, width), BF16),
            jax.ShapeDtypeStruct((fan, nodes, width), F32),
            jax.ShapeDtypeStruct((nodes, width), BF16),
        ],
        scratch_shapes=[pltpu.VMEM((width // 128, fan * TILE, 128), F32)],
        compiler_params=params(),
        name="base_terms",
    )(edge, grid, cot, w_edge, w_dst, w_out, bias)


def column_kernel(
    fan, base, planes, d_agg, grid, cot, src, src_t, low, own, high, w_src,
    packed, d_node, sums, proj, acc, g_edge, g_dst, g_out, g_bias,
):
    step = pl.program_id(0)
    width = grid.shape[1]
    owned = own.shape[0]
    outs = cot.shape[1]

    @pl.when(step == 0)
    def _():
        for j, part in enumerate((low, own, high)):
            proj[j * owned : (j + 1) * owned] = dot(part[...], w_src[...]).astype(BF16)
        for total in (acc, g_edge, g_dst, g_out, g_bias):
            total[...] = jnp.zeros_like(total)

    rows = grid.shape[0]
    near = 3 * owned
    upstream = d_agg[...].astype(F32)
    silu_sum = jnp.zeros(upstream.shape, F32)
    node_sum = jnp.zeros(upstream.shape, F32)
    for k in range(fan):
        hit = lax.broadcasted_iota(jnp.int32, (rows, near), 1) == src[:, k : k + 1]
        pick = jnp.where(hit, 1.0, 0.0).astype(BF16)
        pre = base[k] + dot(pick, proj[...])
        sig = 0.5 + 0.5 * jnp.tanh(0.5 * pre)
        silu = pre * sig
        silu_sum += silu
        d_pre = (upstream * (sig + silu * (1.0 - sig))).astype(BF16)
        node_sum += d_pre.astype(F32)
        hit_t = lax.broadcasted_iota(jnp.int32, (near, rows), 0) == src_t[k : k + 1, :]
        pick_t = jnp.where(hit_t, 1.0, 0.0).astype(BF16)
        acc[...] += dot(pick_t, d_pre)
        g_edge[...] += dot(planes[k], d_pre, TN)
    agg = silu_sum.astype(BF16)
    node = node_sum.astype(BF16)
    d_node[...] = node
    g_out[...] += dot(cot[...], agg, TN)
    g_dst[...] += dot(grid[...], node, TN)
    g_bias[...] += jnp.sum(node_sum.reshape(rows // 8, 8, node_sum.shape[1]), axis=0)

    @pl.when(step == pl.num_programs(0) - 1)
    def _():
        total = acc[...].astype(BF16)
        sums[...] = total
        g_src = jnp.zeros(g_edge.shape, F32)
        for j, part in enumerate((low, own, high)):
            g_src += dot(part[...], total[j * owned : (j + 1) * owned], TN)
        packed[0:width] = g_src.astype(BF16)
        packed[width : 2 * width] = g_edge[...].astype(BF16)
        packed[2 * width : 3 * width] = g_dst[...].astype(BF16)
        tail = packed.shape[0] - 3 * width
        bias_row = jnp.sum(g_bias[...], axis=0, keepdims=True)
        place = lax.broadcasted_iota(jnp.int32, (tail, bias_row.shape[1]), 0)
        out_rows = jnp.concatenate(
            [g_out[...], jnp.zeros((tail - g_out.shape[0], bias_row.shape[1]), F32)], axis=0
        )
        packed[3 * width :] = jnp.where(place == outs, bias_row, out_rows).astype(BF16)


def column_call(h, parts, base, planes, d_agg, grid, cot, src, src_t, low, own, high, w_src, rows):
    fan, nodes, width = planes.shape
    cols = width // parts
    outs = cot.shape[1]
    owned = own.shape[0]
    near = 3 * owned
    whole = lambda *shape: pl.BlockSpec(shape, lambda i: (0,) * len(shape))
    return pl.pallas_call(
        functools.partial(column_kernel, fan),
        grid=(nodes // TILE,),
        in_specs=[
            pl.BlockSpec((fan, TILE, cols), lambda i: (0, i, h)),
            pl.BlockSpec((fan, TILE, width), lambda i: (0, i, 0)),
            pl.BlockSpec((TILE, cols), lambda i: (i, h)),
            pl.BlockSpec((TILE, width), lambda i: (i, 0)),
            pl.BlockSpec((TILE, outs), lambda i: (i, 0)),
            pl.BlockSpec((TILE, fan), lambda i: (i, 0)),
            pl.BlockSpec((fan, TILE), lambda i: (0, i)),
            whole(owned, width),
            whole(owned, width),
            whole(owned, width),
            pl.BlockSpec((width, cols), lambda i: (0, h)),
        ],
        out_specs=[
            whole(rows, cols),
            pl.BlockSpec((TILE, cols), lambda i: (i, 0)),
            whole(near, cols),
        ],
        out_shape=[
            jax.ShapeDtypeStruct((rows, cols), BF16),
            jax.ShapeDtypeStruct((nodes, cols), BF16),
            jax.ShapeDtypeStruct((near, cols), BF16),
        ],
        scratch_shapes=[
            pltpu.VMEM((near, cols), BF16),
            pltpu.VMEM((near, cols), F32),
            pltpu.VMEM((width, cols), F32),
            pltpu.VMEM((width, cols), F32),
            pltpu.VMEM((outs, cols), F32),
            pltpu.VMEM((8, cols), F32),
        ],
        compiler_params=params(),
        name=f"columns_{h}",
    )(base, planes, d_agg, grid, cot, src, src_t, low, own, high, w_src)


def exchanged(block, partner_of):
    regions = lax.axis_size("region")
    return lax.ppermute(block, "region", [(i, partner_of(i)) for i in range(regions)])


def orders(regions):
    bits = [1 << b for b in range(1, regions.bit_length() - 1)]
    other = list(bits)
    if len(other) > 1:
        other[0], other[1] = other[1], other[0]
    return [1] + bits, [1] + other


def total_over_regions(block):
    regions = lax.axis_size("region")
    here = lax.axis_index("region")
    even, odd = orders(regions)
    stages = []
    for a, b in zip(even, odd):
        side = jnp.where(here % 2 == 0, (here // a) % 2, (here // b) % 2)
        stages.append((side, lambda i, a=a, b=b: i ^ (b if i % 2 else a)))
    for side, partner in stages:
        half = block.shape[0] // 2
        send = lax.dynamic_slice_in_dim(block, (1 - side) * half, half, 0).astype(BF16)
        arrived = exchanged(send, partner)
        keep = lax.dynamic_slice_in_dim(block, side * half, half, 0)
        block = keep.astype(F32) + arrived.astype(F32)
    block = block.astype(BF16)
    for side, partner in reversed(stages):
        arrived = exchanged(block, partner)
        block = jnp.where(
            side == 0, jnp.concatenate([block, arrived]), jnp.concatenate([arrived, block])
        )
    return block


def ring(regions, distance):
    return lambda i: (i + distance) % regions


def shards(
    grid_latent, edge_latent, mesh_latent, sources, w_src, w_edge, w_dst, bias, w_out, cotangent
):
    owned, width = mesh_latent.shape
    outs = cotangent.shape[1]
    regions = lax.axis_size("region")
    here = lax.axis_index("region")
    low = exchanged(mesh_latent, ring(regions, 1))
    high = exchanged(mesh_latent, ring(regions, -1))
    local = jnp.mod(sources - (here - 1) * owned, owned * regions)
    base, planes, d_agg = None, None, None
    planes, base, d_agg = base_call(
        edge_latent, grid_latent, cotangent, w_edge, w_dst, w_out, bias.reshape(1, -1)
    )
    unit = 8 * regions
    rows = -(-(3 * width + outs + 1) // unit) * unit
    parts = 2
    packed, d_node, sums = [], [], []
    for h in range(parts):
        a, b, c = column_call(
            h, parts, base, planes, d_agg, grid_latent, cotangent, local, local.T,
            low, mesh_latent, high, w_src, rows,
        )
        packed.append(a)
        d_node.append(b)
        sums.append(c)
    totals = [total_over_regions(block) for block in packed]
    sums = jnp.concatenate(sums, axis=1)
    d_mesh_in = (
        sums[owned : 2 * owned].astype(F32)
        + exchanged(sums[:owned], ring(regions, -1)).astype(F32)
        + exchanged(sums[2 * owned :], ring(regions, 1)).astype(F32)
    ).astype(BF16)
    d_mesh = dot(d_mesh_in, w_src, NT)
    d_grid = dot(jnp.concatenate(d_node, axis=1), w_dst, NT).astype(BF16)
    total = jnp.concatenate(totals, axis=1).astype(F32)
    return (
        d_grid,
        d_mesh,
        total[:width],
        total[width : 2 * width],
        total[2 * width : 3 * width],
        total[3 * width + outs],
        total[3 * width : 3 * width + outs].T,
    )


def solution(mesh):
    placed = (
        P(("member", "region"), None),
        P(("member", "region"), None),
        P(("member", "region"), None),
        P("region", None),
        P(),
        P(),
        P(),
        P(),
        P(),
        P(("member", "region"), None),
    )
    return jax.shard_map(
        shards,
        mesh=mesh,
        in_specs=placed,
        out_specs=(
            P(("member", "region"), None),
            P(("member", "region"), None),
            P("member", None),
            P("member", None),
            P("member", None),
            P("member"),
            P("member", None),
        ),
        check_vma=False,
    )
```

```python
import functools

import jax
import jax.numpy as jnp
from jax import lax
from jax.experimental import pallas as pl
from jax.experimental.pallas import tpu as pltpu
from jax.sharding import PartitionSpec as P

BF16 = jnp.bfloat16
F32 = jnp.float32
BASE_TILE = 256
TILE = 512
NT = (((1,), (1,)), ((), ()))
TN = (((0,), (0,)), ((), ()))
VMEM_LIMIT = 60 * 1024 * 1024
HBM = pl.BlockSpec(memory_space=pltpu.HBM)
VMEM = pl.BlockSpec(memory_space=pltpu.VMEM)


def dot(a, b, dims=(((1,), (0,)), ((), ()))):
    return lax.dot_general(a, b, dims, preferred_element_type=F32)


def params():
    return pltpu.CompilerParams(vmem_limit_bytes=VMEM_LIMIT)


def copies(sems, pairs):
    made = [pltpu.make_async_copy(a, b, sems.at[i]) for i, (a, b) in enumerate(pairs)]
    for copy in made:
        copy.start()
    return made


def base_kernel(
    parts, tiles, edge_h, grid_h, cot_h, w_edge_h, w_dst_h, w_out_h, bias,
    planes_h, base_h, d_agg_h,
    edge, grid, cot, w_edge, w_dst, w_out, planes, base, d_agg, wide, node, sems, in_sems, out_sems,
):
    nodes, width = grid.shape
    fan = planes.shape[0]
    cols = width // parts
    rows = nodes // tiles
    chunk = wide.shape[2]
    arriving = []
    for i in range(tiles):
        e = slice(i * fan * rows, (i + 1) * fan * rows)
        g = slice(i * rows, (i + 1) * rows)
        arriving.append(
            copies(in_sems.at[i], ((edge_h.at[e, :], edge.at[e, :]), (grid_h.at[g, :], grid.at[g, :])))
        )
        if i == 0:
            weights = copies(
                sems, ((w_dst_h, w_dst), (w_edge_h, w_edge), (w_out_h, w_out), (cot_h, cot))
            )
    leaving = []
    for i in range(tiles):
        e = slice(i * fan * rows, (i + 1) * fan * rows)
        g = slice(i * rows, (i + 1) * rows)
        for copy in arriving[i]:
            copy.wait()
        for c in range(wide.shape[0]):
            wide[c] = edge[e, c * chunk : (c + 1) * chunk].astype(F32)
        for k in range(fan):
            for c in range(wide.shape[0]):
                piece = wide[c, pl.ds(k, rows, stride=fan), :]
                planes[k, g, c * chunk : (c + 1) * chunk] = piece.astype(BF16)
        if i == 0:
            for copy in weights:
                copy.wait()
        node[...] = dot(grid[g, :], w_dst[...]) + bias[...]
        product = dot(planes[:, g, :].reshape(fan * rows, width), w_edge[...])
        upstream = dot(cot[:, g], w_out[...], TN).astype(BF16)
        for h in range(parts):
            lanes = slice(h * cols, (h + 1) * cols)
            d_agg[h, g, :] = upstream[:, lanes]
            for k in range(fan):
                base[h, k, g, :] = product[k * rows : (k + 1) * rows, lanes] + node[:, lanes]
        leaving += copies(
            out_sems.at[i],
            (
                (planes.at[:, g, :], planes_h.at[:, g, :]),
                (base.at[:, :, g, :], base_h.at[:, :, g, :]),
                (d_agg.at[:, g, :], d_agg_h.at[:, g, :]),
            ),
        )
    for copy in leaving:
        copy.wait()


def base_call(parts, edge, grid, cot_t, w_edge, w_dst, w_out_t, bias):
    nodes, width = grid.shape
    fan = edge.shape[0] // nodes
    outs = cot_t.shape[0]
    cols = width // parts
    tiles = nodes // BASE_TILE
    results = (
        ((fan, nodes, width), BF16),
        ((parts, fan, nodes, cols), F32),
        ((parts, nodes, cols), BF16),
    )
    return pl.pallas_call(
        functools.partial(base_kernel, parts, tiles),
        in_specs=[HBM] * 6 + [VMEM],
        out_specs=[HBM] * 3,
        out_shape=[jax.ShapeDtypeStruct(*result) for result in results],
        scratch_shapes=[
            pltpu.VMEM(edge.shape, BF16),
            pltpu.VMEM(grid.shape, BF16),
            pltpu.VMEM((outs, nodes), BF16),
            pltpu.VMEM((width, width), BF16),
            pltpu.VMEM((width, width), BF16),
            pltpu.VMEM((outs, width), BF16),
        ]
        + [pltpu.VMEM(*result) for result in results]
        + [
            pltpu.VMEM((width // 128, fan * BASE_TILE, 128), F32),
            pltpu.VMEM((BASE_TILE, width), F32),
            pltpu.SemaphoreType.DMA((4,)),
            pltpu.SemaphoreType.DMA((tiles, 2)),
            pltpu.SemaphoreType.DMA((tiles, 3)),
        ],
        compiler_params=params(),
        name="base_terms",
    )(edge, grid, cot_t, w_edge, w_dst, w_out_t, bias)


def column_kernel(
    h, tiles, planes_h, base_h, d_agg_h, grid_h, cot_h, src, low_h, own_h, high_h, w_src_h,
    packed, d_node, sums,
    planes, base, d_agg, grid, cot, near_rows, w_src, proj, *rest,
):
    pick, pick_t, d_pre = rest[:tiles], rest[tiles : 2 * tiles], rest[2 * tiles : 3 * tiles]
    g_edge, g_dst, g_out, g_bias, acc, sems, tile_sems = rest[3 * tiles :]
    fan, nodes, width = planes.shape
    owned = own_h.shape[0]
    outs, cols = g_out.shape
    rows = nodes // tiles
    lanes = pl.ds(h * cols, cols)
    started = copies(
        sems,
        [(w_src_h.at[:, lanes], w_src)]
        + [(part, near_rows.at[j]) for j, part in enumerate((low_h, own_h, high_h))]
        + [(d_agg_h.at[h], d_agg), (cot_h, cot), (grid_h, grid)],
    )
    arriving = []
    for i in range(tiles):
        g = slice(i * rows, (i + 1) * rows)
        arriving.append(
            copies(
                tile_sems.at[i],
                (
                    (base_h.at[h, :, g, :], base.at[:, g, :]),
                    (planes_h.at[:, g, :], planes.at[:, g, :]),
                ),
            )
        )
    regions = lax.axis_size("region")
    first = (lax.axis_index("region") - 1) * owned
    one, zero = jnp.ones((), BF16), jnp.zeros((), BF16)
    across = lax.broadcasted_iota(jnp.int32, (rows, owned), 1).astype(F32).astype(BF16)
    down = lax.broadcasted_iota(jnp.int32, (owned, rows), 0).astype(F32).astype(BF16)

    def picks(i):
        local = src[:, i * rows : (i + 1) * rows] - first
        local = jnp.where(local < 0, local + owned * regions, local)
        local = jnp.where(local >= owned * regions, local - owned * regions, local).astype(F32)
        tall = jnp.transpose(jnp.concatenate([local, jnp.zeros((8 - fan, rows), F32)], axis=0))
        for k in range(fan):
            for j in range(3):
                place = (tall[:, k : k + 1] - float(j * owned)).astype(BF16)
                pick[i][k * rows : (k + 1) * rows, j * owned : (j + 1) * owned] = jnp.where(
                    across == place, one, zero
                )
                place = (local[k : k + 1, :] - float(j * owned)).astype(BF16)
                pick_t[i][j * owned : (j + 1) * owned, k * rows : (k + 1) * rows] = jnp.where(
                    down == place, one, zero
                )

    def add(total, i, term):
        if i == 0:
            total[...] = term
        else:
            total[...] += term

    picks(0)
    for copy in started[:4]:
        copy.wait()
    for j in range(3):
        proj[j * owned : (j + 1) * owned] = dot(near_rows[j], w_src[...]).astype(BF16)
    for copy in started[4:]:
        copy.wait()
    for i in range(tiles):
        g = slice(i * rows, (i + 1) * rows)
        for copy in arriving[i]:
            copy.wait()
        pre = base[:, g, :].reshape(fan * rows, cols) + dot(pick[i][...], proj[...])
        if i + 1 < tiles:
            picks(i + 1)
        upstream = d_agg[g, :].astype(F32)
        silu_sum = node_sum = None
        for k in range(fan):
            part = slice(k * rows, (k + 1) * rows)
            sig = 0.5 + 0.5 * jnp.tanh(0.5 * pre[part])
            silu = pre[part] * sig
            term = (upstream * (sig + silu * (1.0 - sig))).astype(BF16)
            d_pre[i][part] = term
            silu_sum = silu if k == 0 else silu_sum + silu
            node_sum = term.astype(F32) if k == 0 else node_sum + term.astype(F32)
        agg = silu_sum.astype(BF16)
        node = node_sum.astype(BF16)
        d_node[g, :] = node
        add(acc, i, dot(pick_t[i][...], d_pre[i][...]))
        add(g_edge, i, dot(planes[:, g, :].reshape(fan * rows, width), d_pre[i][...], TN))
        add(g_out, i, dot(cot[:, g], agg))
        add(g_dst, i, dot(grid[g, :], node, TN))
        add(g_bias, i, jnp.sum(node_sum.reshape(rows // 8, 8, cols), axis=0))
    total = acc[...].astype(BF16)
    sums[...] = total
    near_all = near_rows[...].reshape(3 * owned, width)
    packed[0:width] = dot(near_all, total, TN).astype(BF16)
    packed[width : 2 * width] = g_edge[...].astype(BF16)
    packed[2 * width : 3 * width] = g_dst[...].astype(BF16)
    tail = packed.shape[0] - 3 * width
    bias_row = jnp.sum(g_bias[...], axis=0, keepdims=True)
    place = lax.broadcasted_iota(jnp.int32, (tail, cols), 0)
    out_rows = jnp.concatenate([g_out[...], jnp.zeros((tail - outs, cols), F32)], axis=0)
    packed[3 * width :] = jnp.where(place == outs, bias_row, out_rows).astype(BF16)


def column_call(h, parts, planes, base, d_agg, grid, cot_t, src_t, low, own, high, w_src, rows):
    fan, nodes, width = planes.shape
    cols = width // parts
    outs = cot_t.shape[0]
    owned = own.shape[0]
    near = 3 * owned
    tiles = nodes // TILE
    return pl.pallas_call(
        functools.partial(column_kernel, h, tiles),
        in_specs=[HBM] * 5 + [VMEM] + [HBM] * 4,
        out_specs=[VMEM] * 3,
        out_shape=[
            jax.ShapeDtypeStruct((rows, cols), BF16),
            jax.ShapeDtypeStruct((nodes, cols), BF16),
            jax.ShapeDtypeStruct((near, cols), BF16),
        ],
        scratch_shapes=[
            pltpu.VMEM((fan, nodes, width), BF16),
            pltpu.VMEM((fan, nodes, cols), F32),
            pltpu.VMEM((nodes, cols), BF16),
            pltpu.VMEM((nodes, width), BF16),
            pltpu.VMEM((outs, nodes), BF16),
            pltpu.VMEM((3, owned, width), BF16),
            pltpu.VMEM((width, cols), BF16),
            pltpu.VMEM((near, cols), BF16),
        ]
        + [pltpu.VMEM((fan * TILE, near), BF16)] * tiles
        + [pltpu.VMEM((near, fan * TILE), BF16)] * tiles
        + [pltpu.VMEM((fan * TILE, cols), BF16)] * tiles
        + [
            pltpu.VMEM((width, cols), F32),
            pltpu.VMEM((width, cols), F32),
            pltpu.VMEM((outs, cols), F32),
            pltpu.VMEM((8, cols), F32),
            pltpu.VMEM((near, cols), F32),
            pltpu.SemaphoreType.DMA((7,)),
            pltpu.SemaphoreType.DMA((tiles, 2)),
        ],
        compiler_params=params(),
        name=f"columns_{h}",
    )(planes, base, d_agg, grid, cot_t, src_t, low, own, high, w_src)


def exchanged(block, partner_of):
    regions = lax.axis_size("region")
    return lax.ppermute(block, "region", [(i, partner_of(i)) for i in range(regions)])


def orders(regions):
    bits = [1 << b for b in range(1, regions.bit_length() - 1)]
    other = list(bits)
    if len(other) > 1:
        other[0], other[1] = other[1], other[0]
    return [1] + bits, [1] + other


def total_over_regions(block):
    regions = lax.axis_size("region")
    here = lax.axis_index("region")
    even, odd = orders(regions)
    stages = []
    for a, b in zip(even, odd):
        side = jnp.where(here % 2 == 0, (here // a) % 2, (here // b) % 2)
        stages.append((side, lambda i, a=a, b=b: i ^ (b if i % 2 else a)))
    last_side, last_partner = stages.pop()
    for side, partner in stages:
        half = block.shape[0] // 2
        send = lax.dynamic_slice_in_dim(block, (1 - side) * half, half, 0).astype(BF16)
        arrived = exchanged(send, partner)
        keep = lax.dynamic_slice_in_dim(block, side * half, half, 0)
        block = keep.astype(F32) + arrived.astype(F32)
    block = block.astype(BF16)
    block = (block.astype(F32) + exchanged(block, last_partner).astype(F32)).astype(BF16)
    for side, partner in reversed(stages):
        arrived = exchanged(block, partner)
        block = jnp.where(
            side == 0, jnp.concatenate([block, arrived]), jnp.concatenate([arrived, block])
        )
    return block


def ring(regions, distance):
    return lambda i: (i + distance) % regions


def shards(
    grid_latent, edge_latent, mesh_latent, sources, w_src, w_edge, w_dst, bias, w_out, cotangent
):
    owned, width = mesh_latent.shape
    outs = cotangent.shape[1]
    regions = lax.axis_size("region")
    low = exchanged(mesh_latent, ring(regions, 1))
    high = exchanged(mesh_latent, ring(regions, -1))
    cot_t, src_t = cotangent.T, sources.T
    parts = 2
    planes, base, d_agg = base_call(
        parts, edge_latent, grid_latent, cot_t, w_edge, w_dst, w_out.T, bias.reshape(1, -1)
    )
    unit = 8 * regions
    rows = -(-(3 * width + outs + 1) // unit) * unit
    packed, d_node, sums = [], [], []
    for h in range(parts):
        a, b, c = column_call(
            h, parts, planes, base, d_agg, grid_latent, cot_t, src_t,
            low, mesh_latent, high, w_src, rows,
        )
        packed.append(a)
        d_node.append(b)
        sums.append(c)
    totals = [total_over_regions(block) for block in packed]
    sums = jnp.concatenate(sums, axis=1)
    d_mesh_in = (
        sums[owned : 2 * owned].astype(F32)
        + exchanged(sums[:owned], ring(regions, -1)).astype(F32)
        + exchanged(sums[2 * owned :], ring(regions, 1)).astype(F32)
    ).astype(BF16)
    d_mesh = dot(d_mesh_in, w_src, NT)
    d_grid = dot(jnp.concatenate(d_node, axis=1), w_dst, NT).astype(BF16)
    total = jnp.concatenate(totals, axis=1).astype(F32)
    return (
        d_grid,
        d_mesh,
        total[:width],
        total[width : 2 * width],
        total[2 * width : 3 * width],
        total[3 * width + outs],
        total[3 * width : 3 * width + outs].T,
    )


def solution(mesh):
    placed = (
        P(("member", "region"), None),
        P(("member", "region"), None),
        P(("member", "region"), None),
        P("region", None),
        P(),
        P(),
        P(),
        P(),
        P(),
        P(("member", "region"), None),
    )
    return jax.shard_map(
        shards,
        mesh=mesh,
        in_specs=placed,
        out_specs=(
            P(("member", "region"), None),
            P(("member", "region"), None),
            P("member", None),
            P("member", None),
            P("member", None),
            P("member"),
            P("member", None),
        ),
        check_vma=False,
    )
```

```python
import functools

import jax
import jax.numpy as jnp
from jax import lax
from jax.experimental import pallas as pl
from jax.experimental.pallas import tpu as pltpu
from jax.sharding import PartitionSpec as P

BF16 = jnp.bfloat16
F32 = jnp.float32
TILE = 512
NT = (((1,), (1,)), ((), ()))
TN = (((0,), (0,)), ((), ()))
VMEM_LIMIT = 60 * 1024 * 1024
HBM = pl.BlockSpec(memory_space=pltpu.HBM)
VMEM = pl.BlockSpec(memory_space=pltpu.VMEM)


def dot(a, b, dims=(((1,), (0,)), ((), ()))):
    return lax.dot_general(a, b, dims, preferred_element_type=F32)


def params():
    return pltpu.CompilerParams(vmem_limit_bytes=VMEM_LIMIT)


def copies(sems, pairs):
    made = [pltpu.make_async_copy(a, b, sems.at[i]) for i, (a, b) in enumerate(pairs)]
    for copy in made:
        copy.start()
    return made


def places(src, owned):
    regions = lax.axis_size("region")
    local = src - (lax.axis_index("region") - 1) * owned
    local = jnp.where(local < 0, local + owned * regions, local)
    return jnp.where(local >= owned * regions, local - owned * regions, local).astype(F32)


def one_hot(counter, place):
    return jnp.where(counter == place.astype(BF16), jnp.ones((), BF16), jnp.zeros((), BF16))


def counting(shape, dim):
    return lax.broadcasted_iota(jnp.int32, shape, dim).astype(F32).astype(BF16)


def edge_kernel(
    tiles, edge_h, grid_h, cot_h, src_h, own_h, chip_h, next_h, w_src_h, w_edge_h, w_dst_h, w_out_h, bias_h,
    send_a, keep_a, send_b, keep_b, own_sum_h, to_chip_h, to_next_h, d_node_h,
    edge, grid, cot, src, near_rows, w_src, w_dst, w_out, bias, rhs, wide, pre, node_term, d_pre, d_node, packed, sums, *rest,
):
    lhs, pick_t = rest[:tiles], rest[tiles : 2 * tiles]
    acc, g_edge, g_dst, g_out, g_bias, sems, near_sems, in_sems, out_sems = rest[2 * tiles :]
    nodes, width = grid.shape
    fan = src.shape[0]
    owned = own_h.shape[0]
    outs = cot.shape[0]
    rows = nodes // tiles
    chunk = wide.shape[2]
    regions = lax.axis_size("region")
    region = lax.axis_index("region")
    tile = [slice(i * rows, (i + 1) * rows) for i in range(tiles)]

    odd = region % 2
    arrived = copies(
        near_sems,
        [(own_h, near_rows.at[1]), (chip_h, near_rows.at[2 - 2 * odd]), (next_h, near_rows.at[2 * odd])],
    )
    started = copies(sems.at[0], [(src_h, src), (w_src_h, w_src)])
    arriving = []
    for i, g in enumerate(tile):
        e = slice(i * fan * rows, (i + 1) * fan * rows)
        arriving.append(
            copies(in_sems.at[i], ((edge_h.at[e, :], edge.at[e, :]), (grid_h.at[g, :], grid.at[g, :])))
        )
        if i == 0:
            weights = copies(
                sems.at[1],
                [(w_edge_h, rhs.at[:width, :]), (w_dst_h, w_dst), (w_out_h, w_out)]
                + [(cot_h, cot), (bias_h, bias)],
            )
    across = counting((rows, owned), 1)
    down = counting((owned, rows), 0)

    def picks(i):
        local = places(src[:, tile[i]], owned)
        tall = jnp.transpose(jnp.concatenate([local, jnp.zeros((8 - fan, rows), F32)], axis=0))
        for k in range(fan):
            for j in range(3):
                lanes = slice(width + j * owned, width + (j + 1) * owned)
                lhs[i][k * rows : (k + 1) * rows, lanes] = one_hot(
                    across, tall[:, k : k + 1] - float(j * owned)
                )

    def picks_t(i):
        local = places(src[:, tile[i]], owned)
        for k in range(fan):
            for j in range(3):
                pick_t[i][j * owned : (j + 1) * owned, k * rows : (k + 1) * rows] = one_hot(
                    down, local[k : k + 1, :] - float(j * owned)
                )

    def planes(i):
        e = slice(i * fan * rows, (i + 1) * fan * rows)
        for c in range(wide.shape[0]):
            wide[c] = edge[e, c * chunk : (c + 1) * chunk].astype(F32)
        for k in range(fan):
            for c in range(wide.shape[0]):
                piece = wide[c, pl.ds(k, rows, stride=fan), :]
                lhs[i][k * rows : (k + 1) * rows, c * chunk : (c + 1) * chunk] = piece.astype(BF16)

    def add(total, i, term):
        if i == 0:
            total[...] = term
        else:
            total[...] += term

    started[0].wait()
    for i in range(tiles):
        picks(i)
    started[1].wait()
    for copy in arrived:
        copy.wait()
    rhs[width:] = dot(near_rows[...].reshape(3 * owned, width), w_src[...]).astype(BF16)
    for i, g in enumerate(tile):
        for copy in arriving[i]:
            copy.wait()
        planes(i)
        if i == 0:
            for copy in weights:
                copy.wait()
        node_term[g, :] = dot(grid[g, :], w_dst[...]) + bias[...]
        pre[:, g, :] = dot(lhs[i][...], rhs[...]).reshape(fan, rows, width)
        picks_t(i)
    for i, g in enumerate(tile):
        upstream = dot(cot[:, g], w_out[...], TN).astype(BF16).astype(F32)
        silu_sum = node_sum = None
        for k in range(fan):
            value = pre[k, g, :] + node_term[g, :]
            sig = 0.5 + 0.5 * jnp.tanh(0.5 * value)
            silu = value * sig
            term = (upstream * (sig + silu * (1.0 - sig))).astype(BF16)
            d_pre[k, g, :] = term
            silu_sum = silu if k == 0 else silu_sum + silu
            node_sum = term.astype(F32) if k == 0 else node_sum + term.astype(F32)
        agg = silu_sum.astype(BF16)
        node = node_sum.astype(BF16)
        d_node[g, :] = node
        term = d_pre[:, g, :].reshape(fan * rows, width)
        add(acc, i, dot(pick_t[i][...], term))
        add(g_edge, i, dot(lhs[i][:, :width], term, TN))
        add(g_out, i, dot(cot[:, g], agg))
        add(g_dst, i, dot(grid[g, :], node, TN))
        add(g_bias, i, jnp.sum(node_sum.reshape(rows // 8, 8, width), axis=0))
    total = acc[...].astype(BF16)
    sums[...] = total.reshape(3, owned, width)
    tail = packed.shape[0] - 3 * width
    bias_row = jnp.sum(g_bias[...], axis=0, keepdims=True)
    place = lax.broadcasted_iota(jnp.int32, (tail, width), 0)
    out_rows = jnp.concatenate([g_out[...], jnp.zeros((tail - outs, width), F32)], axis=0)
    packed[:tail] = jnp.where(place == outs, bias_row, out_rows).astype(BF16)
    g_src = dot(near_rows[...].reshape(3 * owned, width), total, TN)
    packed[tail : tail + width] = g_src.astype(BF16)
    packed[tail + width : tail + 2 * width] = g_edge[...].astype(BF16)
    packed[tail + 2 * width :] = g_dst[...].astype(BF16)
    pairs = []
    start = 0
    for send, keep in ((send_a, keep_a), (send_b, keep_b)):
        half = send.shape[0]
        gone = pl.ds(pl.multiple_of(start + (1 - odd) * half, 8), half)
        kept = pl.ds(pl.multiple_of(start + odd * half, 8), half)
        pairs += [(packed.at[gone, :], send), (packed.at[kept, :], keep)]
        start += 2 * half
    pairs += [(sums.at[1], own_sum_h), (sums.at[2 - 2 * odd], to_chip_h)]
    pairs += [(sums.at[2 * odd], to_next_h), (d_node, d_node_h)]
    for copy in copies(out_sems, pairs):
        copy.wait()


def edge_call(edge, grid, cot_t, src_t, near, w_src, w_edge, w_dst, w_out_t, bias, chain_rows):
    nodes, width = grid.shape
    fan, outs = src_t.shape[0], cot_t.shape[0]
    owned = near[0].shape[0]
    reach = 3 * owned
    tiles = nodes // TILE
    halves = [rows // 2 for rows in chain_rows for _ in range(2)]
    shapes = [(rows, width) for rows in halves] + [(owned, width)] * 3 + [(nodes, width)]
    return pl.pallas_call(
        functools.partial(edge_kernel, tiles),
        in_specs=[HBM] * 12,
        out_specs=[HBM] * len(shapes),
        out_shape=[jax.ShapeDtypeStruct(shape, BF16) for shape in shapes],
        scratch_shapes=[
            pltpu.VMEM(edge.shape, BF16),
            pltpu.VMEM((nodes, width), BF16),
            pltpu.VMEM((outs, nodes), BF16),
            pltpu.VMEM((fan, nodes), jnp.int32),
            pltpu.VMEM((3, owned, width), BF16),
            pltpu.VMEM((width, width), BF16),
            pltpu.VMEM((width, width), BF16),
            pltpu.VMEM((outs, width), BF16),
            pltpu.VMEM((1, width), F32),
            pltpu.VMEM((width + reach, width), BF16),
            pltpu.VMEM((width // 128, fan * TILE, 128), F32),
            pltpu.VMEM((fan, nodes, width), F32),
            pltpu.VMEM((nodes, width), F32),
            pltpu.VMEM((fan, nodes, width), BF16),
            pltpu.VMEM((nodes, width), BF16),
            pltpu.VMEM((sum(chain_rows), width), BF16),
            pltpu.VMEM((3, owned, width), BF16),
        ]
        + [pltpu.VMEM((fan * TILE, width + reach), BF16)] * tiles
        + [pltpu.VMEM((reach, fan * TILE), BF16)] * tiles
        + [
            pltpu.VMEM((reach, width), F32),
            pltpu.VMEM((width, width), F32),
            pltpu.VMEM((width, width), F32),
            pltpu.VMEM((outs, width), F32),
            pltpu.VMEM((8, width), F32),
            pltpu.SemaphoreType.DMA((2, 5)),
            pltpu.SemaphoreType.DMA((3,)),
            pltpu.SemaphoreType.DMA((tiles, 2)),
            pltpu.SemaphoreType.DMA((8,)),
        ],
        compiler_params=params(),
        name="edge_terms",
    )(edge, grid, cot_t, src_t, *near, w_src, w_edge, w_dst, w_out_t, bias)


def exchanged(block, pairs):
    return lax.ppermute(block, "region", pairs)


def orders(regions):
    bits = [1 << b for b in range(1, regions.bit_length() - 1)]
    other = list(bits)
    if len(other) > 1:
        other[0], other[1] = other[1], other[0]
    return [1] + bits, [1] + other


def stages_of(regions, here):
    stages = []
    for a, b in zip(*orders(regions)):
        side = jnp.where(here % 2 == 0, (here // a) % 2, (here // b) % 2)
        stages.append((side, [(i, i ^ (b if i % 2 else a)) for i in range(regions)]))
    return stages


def neighbours(regions):
    chip = [(i, i ^ 1) for i in range(regions)]
    return chip, [(i, (i + (1 if i % 2 else -1)) % regions) for i in range(regions)]


def after(value, other):
    corner = other[(slice(0, 1),) * other.ndim].reshape((1,) * value.ndim)
    return value + jnp.minimum(jnp.abs(corner), 0).astype(value.dtype)


class Chain:
    def __init__(self, keep, send, stages):
        self.stages, self.level = stages, 0
        self.block, self.arrived = keep, exchanged(send, stages[0][1])

    def total(self):
        return self.block.astype(F32) + self.arrived.astype(F32)

    def halve(self):
        self.level += 1
        side, partner = self.stages[self.level]
        block = self.total()
        half = block.shape[0] // 2
        send = lax.dynamic_slice_in_dim(block, (1 - side) * half, half, 0).astype(BF16)
        self.block = lax.dynamic_slice_in_dim(block, side * half, half, 0)
        self.arrived = exchanged(send, partner)

    def swap(self, *others):
        self.level += 1
        block = self.total()
        for other in others:
            block = after(block, other)
        self.block = block.astype(BF16)
        self.arrived = exchanged(self.block, self.stages[self.level][1])

    def double(self, *others):
        if self.level == len(self.stages) - 1:
            self.block = self.total().astype(BF16)
        else:
            self.block = self.joined(0, 2 * self.block.shape[0])
        for other in others:
            self.block = after(self.block, other)
        self.level -= 1
        self.arrived = exchanged(self.block, self.stages[self.level][1])

    def joined(self, start, stop):
        low = jnp.concatenate([self.block, self.arrived])[start:stop]
        high = jnp.concatenate([self.arrived, self.block])[start:stop]
        return jnp.where(self.stages[self.level][0] == 0, low, high)


def shards(
    grid_latent, edge_latent, mesh_latent, sources, w_src, w_edge, w_dst, bias, w_out, cotangent
):
    width = mesh_latent.shape[1]
    outs = cotangent.shape[1]
    regions = lax.axis_size("region")
    chip, beyond = neighbours(regions)
    near = (mesh_latent, exchanged(mesh_latent, chip), exchanged(mesh_latent, beyond))
    unit = 4 * regions
    units = -(-(3 * width + outs + 1) // unit)
    chain_rows = [-(-units // 2) * unit, units // 2 * unit]
    stages = stages_of(regions, lax.axis_index("region"))
    send_a, keep_a, send_b, keep_b, own_sum, to_chip, to_next, d_node = edge_call(
        edge_latent, grid_latent, cotangent.T, sources.T, near,
        w_src, w_edge, w_dst, w_out.T, bias.reshape(1, -1), chain_rows,
    )
    a = Chain(keep_a, send_a, stages)
    b = Chain(keep_b, send_b, stages)
    for level in range(1, len(stages) - 1):
        a.halve()
        b.halve()
    a.swap()
    b.swap()
    from_next = exchanged(after(to_next, a.block), beyond)
    from_chip = exchanged(to_chip, chip)
    d_mesh_in = sum(x.astype(F32) for x in (own_sum, from_chip, from_next))
    d_mesh = dot(d_mesh_in.astype(BF16), w_src, NT)
    d_grid = dot(after(d_node, a.block), w_dst, NT).astype(BF16)
    a.double()
    b.double(d_grid)
    for level in range(2, len(stages) - 1):
        a.double()
        b.double(d_mesh)
    a.double()
    b.double()
    starts = [sum(chain_rows) - i * width for i in (3, 2, 1, 0)]

    def rows_of(start, stop):
        cut = chain_rows[0]
        parts = []
        if start < cut:
            parts.append(a.joined(start, min(stop, cut)))
        if stop > cut:
            parts.append(b.joined(max(start, cut) - cut, stop - cut))
        return jnp.concatenate(parts).astype(F32)

    return (
        d_grid,
        d_mesh,
        rows_of(starts[0], starts[1]),
        rows_of(starts[1], starts[2]),
        rows_of(starts[2], starts[3]),
        rows_of(outs, outs + 1)[0],
        rows_of(0, outs).T,
    )


def solution(mesh):
    placed = (
        P(("member", "region"), None),
        P(("member", "region"), None),
        P(("member", "region"), None),
        P("region", None),
        P(),
        P(),
        P(),
        P(),
        P(),
        P(("member", "region"), None),
    )
    return jax.shard_map(
        shards,
        mesh=mesh,
        in_specs=placed,
        out_specs=(
            P(("member", "region"), None),
            P(("member", "region"), None),
            P("member", None),
            P("member", None),
            P("member", None),
            P("member"),
            P("member", None),
        ),
        check_vma=False,
    )
```

```python
import functools

import jax
import jax.numpy as jnp
from jax import lax
from jax.experimental import pallas as pl
from jax.experimental.pallas import tpu as pltpu
from jax.sharding import PartitionSpec as P

BF16 = jnp.bfloat16
F32 = jnp.float32
TILE = 512
NT = (((1,), (1,)), ((), ()))
TN = (((0,), (0,)), ((), ()))
VMEM_LIMIT = 60 * 1024 * 1024
HBM = pl.BlockSpec(memory_space=pltpu.HBM)
VMEM = pl.BlockSpec(memory_space=pltpu.VMEM)


def dot(a, b, dims=(((1,), (0,)), ((), ()))):
    return lax.dot_general(a, b, dims, preferred_element_type=F32)


def params():
    return pltpu.CompilerParams(vmem_limit_bytes=VMEM_LIMIT)


def copies(sems, pairs):
    made = [pltpu.make_async_copy(a, b, sems.at[i]) for i, (a, b) in enumerate(pairs)]
    for copy in made:
        copy.start()
    return made


def places(src, owned):
    regions = lax.axis_size("region")
    local = src - (lax.axis_index("region") - 1) * owned
    local = jnp.where(local < 0, local + owned * regions, local)
    return jnp.where(local >= owned * regions, local - owned * regions, local).astype(F32)


def one_hot(counter, place):
    return jnp.where(counter == place.astype(BF16), jnp.ones((), BF16), jnp.zeros((), BF16))


def counting(shape, dim):
    return lax.broadcasted_iota(jnp.int32, shape, dim).astype(F32).astype(BF16)


def edge_kernel(
    tiles, edge_h, grid_h, cot_h, src_h, own_h, chip_h, next_h, w_src_h, w_edge_h, w_dst_h, w_out_h, bias_h,
    send_a, keep_a, send_b, keep_b, own_sum, to_chip, to_next, d_node,
    edge, grid, cot, src, near_rows, w_src, w_dst, w_out, bias, rhs, wide, pre, node_term, d_pre, packed, sums, *rest,
):
    lhs, pick_t = rest[:tiles], rest[tiles : 2 * tiles]
    acc, g_edge, g_dst, g_out, g_bias, sems, near_sems, in_sems, out_sems = rest[2 * tiles :]
    nodes, width = grid.shape
    fan = src.shape[0]
    owned = own_h.shape[0]
    outs = cot.shape[0]
    rows = nodes // tiles
    chunk = wide.shape[2]
    regions = lax.axis_size("region")
    region = lax.axis_index("region")
    tile = [slice(i * rows, (i + 1) * rows) for i in range(tiles)]

    odd = region % 2
    arrived = copies(
        near_sems,
        [(own_h, near_rows.at[1]), (chip_h, near_rows.at[2 - 2 * odd]), (next_h, near_rows.at[2 * odd])],
    )
    started = copies(sems.at[0], [(src_h, src), (w_src_h, w_src)])
    arriving = []
    for i, g in enumerate(tile):
        e = slice(i * fan * rows, (i + 1) * fan * rows)
        arriving.append(
            copies(in_sems.at[i], ((edge_h.at[e, :], edge.at[e, :]), (grid_h.at[g, :], grid.at[g, :])))
        )
        if i == 0:
            weights = copies(
                sems.at[1],
                [(w_edge_h, rhs.at[:width, :]), (w_dst_h, w_dst), (w_out_h, w_out)]
                + [(cot_h, cot), (bias_h, bias)],
            )
    across = counting((rows, owned), 1)
    down = counting((owned, rows), 0)

    def picks(i):
        local = places(src[:, tile[i]], owned)
        tall = jnp.transpose(jnp.concatenate([local, jnp.zeros((8 - fan, rows), F32)], axis=0))
        for k in range(fan):
            for j in range(3):
                lanes = slice(width + j * owned, width + (j + 1) * owned)
                lhs[i][k * rows : (k + 1) * rows, lanes] = one_hot(
                    across, tall[:, k : k + 1] - float(j * owned)
                )

    def picks_t(i):
        local = places(src[:, tile[i]], owned)
        for k in range(fan):
            for j in range(3):
                pick_t[i][j * owned : (j + 1) * owned, k * rows : (k + 1) * rows] = one_hot(
                    down, local[k : k + 1, :] - float(j * owned)
                )

    def planes(i):
        e = slice(i * fan * rows, (i + 1) * fan * rows)
        for c in range(wide.shape[0]):
            wide[c] = edge[e, c * chunk : (c + 1) * chunk].astype(F32)
        for k in range(fan):
            for c in range(wide.shape[0]):
                piece = wide[c, pl.ds(k, rows, stride=fan), :]
                lhs[i][k * rows : (k + 1) * rows, c * chunk : (c + 1) * chunk] = piece.astype(BF16)

    def add(total, i, term):
        if i == 0:
            total[...] = term
        else:
            total[...] += term

    started[0].wait()
    for i in range(tiles):
        picks(i)
    started[1].wait()
    for copy in arrived:
        copy.wait()
    rhs[width:] = dot(near_rows[...].reshape(3 * owned, width), w_src[...]).astype(BF16)
    for i, g in enumerate(tile):
        for copy in arriving[i]:
            copy.wait()
        planes(i)
        if i == 0:
            for copy in weights:
                copy.wait()
        node_term[g, :] = dot(grid[g, :], w_dst[...]) + bias[...]
        pre[:, g, :] = dot(lhs[i][...], rhs[...]).reshape(fan, rows, width)
        picks_t(i)
    for i, g in enumerate(tile):
        upstream = dot(cot[:, g], w_out[...], TN).astype(BF16).astype(F32)
        silu_sum = node_sum = None
        for k in range(fan):
            value = pre[k, g, :] + node_term[g, :]
            sig = 0.5 + 0.5 * jnp.tanh(0.5 * value)
            silu = value * sig
            term = (upstream * (sig + silu * (1.0 - sig))).astype(BF16)
            d_pre[k, g, :] = term
            silu_sum = silu if k == 0 else silu_sum + silu
            node_sum = term.astype(F32) if k == 0 else node_sum + term.astype(F32)
        agg = silu_sum.astype(BF16)
        node = node_sum.astype(BF16)
        d_node[g, :] = node
        term = d_pre[:, g, :].reshape(fan * rows, width)
        add(acc, i, dot(pick_t[i][...], term))
        add(g_edge, i, dot(lhs[i][:, :width], term, TN))
        add(g_out, i, dot(cot[:, g], agg))
        add(g_dst, i, dot(grid[g, :], node, TN))
        add(g_bias, i, jnp.sum(node_sum.reshape(rows // 8, 8, width), axis=0))
    total = acc[...].astype(BF16)
    sums[...] = total.reshape(3, owned, width)
    tail = packed.shape[0] - 3 * width
    bias_row = jnp.sum(g_bias[...], axis=0, keepdims=True)
    place = lax.broadcasted_iota(jnp.int32, (tail, width), 0)
    out_rows = jnp.concatenate([g_out[...], jnp.zeros((tail - outs, width), F32)], axis=0)
    packed[:tail] = jnp.where(place == outs, bias_row, out_rows).astype(BF16)
    g_src = dot(near_rows[...].reshape(3 * owned, width), total, TN)
    packed[tail : tail + width] = g_src.astype(BF16)
    packed[tail + width : tail + 2 * width] = g_edge[...].astype(BF16)
    packed[tail + 2 * width :] = g_dst[...].astype(BF16)
    pairs = []
    start = 0
    for send, keep in ((send_a, keep_a), (send_b, keep_b)):
        half = send.shape[0]
        gone = pl.ds(pl.multiple_of(start + (1 - odd) * half, 8), half)
        kept = pl.ds(pl.multiple_of(start + odd * half, 8), half)
        pairs += [(packed.at[gone, :], send), (packed.at[kept, :], keep)]
        start += 2 * half
    pairs += [(sums.at[1], own_sum), (sums.at[2 - 2 * odd], to_chip), (sums.at[2 * odd], to_next)]
    for copy in copies(out_sems, pairs):
        copy.wait()


def edge_call(edge, grid, cot_t, src_t, near, w_src, w_edge, w_dst, w_out_t, bias, chain_rows):
    nodes, width = grid.shape
    fan, outs = src_t.shape[0], cot_t.shape[0]
    owned = near[0].shape[0]
    reach = 3 * owned
    tiles = nodes // TILE
    halves = [rows // 2 for rows in chain_rows for _ in range(2)]
    shapes = [(rows, width) for rows in halves] + [(owned, width)] * 3 + [(nodes, width)]
    return pl.pallas_call(
        functools.partial(edge_kernel, tiles),
        in_specs=[HBM] * 12,
        out_specs=[VMEM] * len(shapes),
        out_shape=[pltpu.VMEM(shape, BF16) for shape in shapes],
        scratch_shapes=[
            pltpu.VMEM(edge.shape, BF16),
            pltpu.VMEM((nodes, width), BF16),
            pltpu.VMEM((outs, nodes), BF16),
            pltpu.VMEM((fan, nodes), jnp.int32),
            pltpu.VMEM((3, owned, width), BF16),
            pltpu.VMEM((width, width), BF16),
            pltpu.VMEM((width, width), BF16),
            pltpu.VMEM((outs, width), BF16),
            pltpu.VMEM((1, width), F32),
            pltpu.VMEM((width + reach, width), BF16),
            pltpu.VMEM((width // 128, fan * TILE, 128), F32),
            pltpu.VMEM((fan, nodes, width), F32),
            pltpu.VMEM((nodes, width), F32),
            pltpu.VMEM((fan, nodes, width), BF16),
            pltpu.VMEM((sum(chain_rows), width), BF16),
            pltpu.VMEM((3, owned, width), BF16),
        ]
        + [pltpu.VMEM((fan * TILE, width + reach), BF16)] * tiles
        + [pltpu.VMEM((reach, fan * TILE), BF16)] * tiles
        + [
            pltpu.VMEM((reach, width), F32),
            pltpu.VMEM((width, width), F32),
            pltpu.VMEM((width, width), F32),
            pltpu.VMEM((outs, width), F32),
            pltpu.VMEM((8, width), F32),
            pltpu.SemaphoreType.DMA((2, 5)),
            pltpu.SemaphoreType.DMA((3,)),
            pltpu.SemaphoreType.DMA((tiles, 2)),
            pltpu.SemaphoreType.DMA((7,)),
        ],
        compiler_params=params(),
        name="edge_terms",
    )(edge, grid, cot_t, src_t, *near, w_src, w_edge, w_dst, w_out_t, bias)


def exchanged(block, pairs):
    return lax.ppermute(block, "region", pairs)


def orders(regions):
    bits = [1 << b for b in range(1, regions.bit_length() - 1)]
    other = list(bits)
    if len(other) > 1:
        other[0], other[1] = other[1], other[0]
    return [1] + bits, [1] + other


def stages_of(regions, here):
    stages = []
    for a, b in zip(*orders(regions)):
        side = jnp.where(here % 2 == 0, (here // a) % 2, (here // b) % 2)
        stages.append((side, [(i, i ^ (b if i % 2 else a)) for i in range(regions)]))
    return stages


def neighbours(regions):
    chip = [(i, i ^ 1) for i in range(regions)]
    return chip, [(i, (i + (1 if i % 2 else -1)) % regions) for i in range(regions)]


def after(value, other):
    nothing = jnp.minimum(jnp.abs(other[:16]), 0).astype(value.dtype)
    return value + jnp.pad(nothing, ((0, value.shape[0] - nothing.shape[0]), (0, 0)))


class Chain:
    def __init__(self, keep, send, stages):
        self.stages, self.level = stages, 0
        self.block, self.arrived = keep, exchanged(send, stages[0][1])

    def total(self):
        return self.block.astype(F32) + self.arrived.astype(F32)

    def halve(self):
        self.level += 1
        side, partner = self.stages[self.level]
        block = self.total()
        half = block.shape[0] // 2
        send = lax.dynamic_slice_in_dim(block, (1 - side) * half, half, 0).astype(BF16)
        self.block = lax.dynamic_slice_in_dim(block, side * half, half, 0)
        self.arrived = exchanged(send, partner)

    def swap(self, *others):
        self.level += 1
        block = self.total()
        for other in others:
            block = after(block, other)
        self.block = block.astype(BF16)
        self.arrived = exchanged(self.block, self.stages[self.level][1])

    def double(self, *others):
        if self.level == len(self.stages) - 1:
            self.block = self.total().astype(BF16)
        else:
            self.block = self.joined(0, 2 * self.block.shape[0])
        for other in others:
            self.block = after(self.block, other)
        self.level -= 1
        self.arrived = exchanged(self.block, self.stages[self.level][1])

    def joined(self, start, stop):
        low = jnp.concatenate([self.block, self.arrived])[start:stop]
        high = jnp.concatenate([self.arrived, self.block])[start:stop]
        return jnp.where(self.stages[self.level][0] == 0, low, high)


def shards(
    grid_latent, edge_latent, mesh_latent, sources, w_src, w_edge, w_dst, bias, w_out, cotangent
):
    width = mesh_latent.shape[1]
    outs = cotangent.shape[1]
    regions = lax.axis_size("region")
    chip, beyond = neighbours(regions)
    near = (mesh_latent, exchanged(mesh_latent, chip), exchanged(mesh_latent, beyond))
    unit = 4 * regions
    units = -(-(3 * width + outs + 1) // unit)
    chain_rows = [-(-units // 2) * unit, units // 2 * unit]
    stages = stages_of(regions, lax.axis_index("region"))
    send_a, keep_a, send_b, keep_b, own_sum, to_chip, to_next, d_node = edge_call(
        edge_latent, grid_latent, cotangent.T, sources.T, near,
        w_src, w_edge, w_dst, w_out.T, bias.reshape(1, -1), chain_rows,
    )
    a = Chain(keep_a, send_a, stages)
    b = Chain(keep_b, send_b, stages)
    for level in range(1, len(stages) - 1):
        a.halve()
        b.halve()
    from_next = exchanged(after(to_next, a.block), beyond)
    a.swap()
    b.swap()
    from_chip = exchanged(to_chip, chip)
    d_mesh_in = sum(x.astype(F32) for x in (own_sum, from_chip, from_next))
    d_mesh = dot(d_mesh_in.astype(BF16), w_src, NT)
    d_grid = dot(after(d_node, a.block), w_dst, NT).astype(BF16)
    for level in range(1, len(stages) - 1):
        a.double(b.block)
    b.double(a.block, d_grid)
    for level in range(2, len(stages) - 1):
        b.double()
    starts = [sum(chain_rows) - i * width for i in (3, 2, 1, 0)]
    a.double(b.block, d_mesh)
    d_w_src = a.joined(starts[0], starts[1]).astype(F32)
    b.double(d_w_src)

    def rows_of(start, stop):
        cut = chain_rows[0]
        parts = []
        if start < cut:
            parts.append(a.joined(start, min(stop, cut)))
        if stop > cut:
            parts.append(b.joined(max(start, cut) - cut, stop - cut))
        return jnp.concatenate(parts).astype(F32)

    return (
        d_grid,
        d_mesh,
        d_w_src,
        rows_of(starts[1], starts[2]),
        rows_of(starts[2], starts[3]),
        rows_of(outs, outs + 1)[0],
        rows_of(0, outs).T,
    )


def solution(mesh):
    placed = (
        P(("member", "region"), None),
        P(("member", "region"), None),
        P(("member", "region"), None),
        P("region", None),
        P(),
        P(),
        P(),
        P(),
        P(),
        P(("member", "region"), None),
    )
    return jax.shard_map(
        shards,
        mesh=mesh,
        in_specs=placed,
        out_specs=(
            P(("member", "region"), None),
            P(("member", "region"), None),
            P("member", None),
            P("member", None),
            P("member", None),
            P("member"),
            P("member", None),
        ),
        check_vma=False,
    )
```
